32 devices in a mesh: tiles: 8 (over y, x, core), lev: 4 (over z).
Axes of the slice: x: 2, y: 2, z: 4, core: 2. Of those that a mesh axis runs over, the one named last changes fastest.
Arguments:
- u_vel: float32 [128, 8, 8100], P('tiles', 'lev'), may hold values from -6 to 6
- v_vel: float32 [128, 8, 8100], P('tiles', 'lev'), may hold values from -6 to 6
- w_vel: float32 [128, 8, 8100], P('tiles', 'lev'), may hold values from -6 to 6
- owner_dev: int32 [128, 4, 1], P('tiles'), may hold values from 0 to 7; in each aligned block of 64 rows (0 to 63, 64 to 127, ..., all dimensions but the last counted through in order) at most 16 rows name the same one
- owner_slot: int32 [128, 4], P('tiles'), may hold values from 0 to 15
- rotation: int32 [128, 4], P('tiles'), may hold values from 0 to 3
- coast: int32 [128, 4], P('tiles'), may hold values 0 or 1
- live: int32 [128], P('tiles'), may hold values 0 or 1
Outputs:
- flux: float32 [128, 8100], P('tiles')
The draws below stay inside these ranges and needn't reach their ends.
Inputs may be any that keep to these rules, and one draw needn't show every extreme that they name: `owner_dev`: among the 4 x 16 sides of the tiles of one index of tiles, no index is named more than 16 times, a bound that some block reaches.
All inputs are finite; a program needn't handle non-finite values. No bound on the sum of `coast` or of `live` on one device may be relied on, other than what follows from the above.
Results may differ from the reference program's by a relative error of at most 0.0003.
Values sent between devices are 32-bit elements; how exact they have to be, the bound alone decides.
A program may use at most 128 MiB of HBM per device.

```python
import math
import jax
import jax.numpy as jnp
import numpy as np
from jax import lax

TS = 90
SLOTS = 16
CELLS = 8100
NTILE = 128
LEVELS = 8
CAP = 16
N_TILES = 8


def set_ends(values, stream_key, low, high):
    longest = values.shape.index(max(values.shape))
    spots = []
    for shift in (0, 1):
        where = [jax.random.randint(jax.random.fold_in(stream_key, axis), (), 0, length) for axis, length in enumerate(values.shape)]
        where[longest] = (where[longest] + shift) % values.shape[longest]
        spots.append(tuple(where))
    return values.at[spots[0]].set(low).at[spots[1]].set(high)


def block_scale(own_key, extent, pieces, least, high):
    loudness = 1.0
    for dim, shards_of in pieces:
        draws = jax.random.uniform(jax.random.fold_in(jax.random.fold_in(own_key, 6), dim), (shards_of,), jnp.float32, least / len(pieces), high / len(pieces))
        loudness = loudness * jnp.repeat(jnp.exp(draws), extent[dim] // shards_of).reshape((-1,) + (1,) * (len(extent) - 1 - dim))
    return loudness


def deal_out(key, own, number, rows, count, top, reach, skew):
    order = jax.random.permutation(key, count)
    crowded, usual = load_shares(count, rows * top, reach, skew, True), load_shares(count, rows * top, reach, skew, False)
    places = jnp.arange(count)

    def named(tallies, turn):
        used = int((tallies > 0).sum())
        fixed = max(1, used // 4)
        shifted = fixed + (places - fixed + turn * (used - fixed)) % max(1, count - fixed)
        return jnp.zeros((count,), jnp.int32).at[order[jnp.where(places < fixed, places, shifted)]].set(jnp.asarray(tallies, jnp.int32))

    tallies = jnp.where(number % 4 == 0, named(crowded, number // 4), named(usual, number - number // 4 - 1))
    mixed = jax.random.permutation(jax.random.fold_in(own, 3), count)
    donor, taker = mixed[0:count // 2 * 2:2], mixed[1:count // 2 * 2:2]
    slack = jnp.minimum(tallies[donor] - 1, reach - tallies[taker]) // 2
    slack = jnp.where((donor == order[0]) | (taker == order[0]) | (tallies[taker] == 0), 0, jnp.maximum(slack, 0))
    shifted = jax.random.randint(jax.random.fold_in(own, 4), (count // 2,), 0, 1 << 20) % (slack + 1)
    tallies = tallies.at[donor].add(-shifted).at[taker].add(shifted)
    labels = jnp.searchsorted(jnp.cumsum(tallies), jnp.arange(rows * top), side="right").astype(jnp.int32)
    grid = labels.reshape(top, rows).T
    grid = grid[jax.random.permutation(jax.random.fold_in(own, 1), rows)]
    turn = jax.random.randint(jax.random.fold_in(own, 2), (rows, 1), 0, top)
    return jnp.take_along_axis(grid, (jnp.arange(top)[None, :] + turn) % top, axis=1)


def load_shares(amount, total, most, slope, full):
    portions = [(1 << 20) // math.isqrt(rank ** slope) + 1 for rank in range(1, amount + 1)]
    largest = most if full else min(most, max(-(-total // amount), total * portions[0] // sum(portions)))
    least = 1 if total - largest >= amount - 1 else 0
    given, rest = [largest] + [least] * (amount - 1), total - largest - least * (amount - 1)
    while rest > 0:
        free = [i for i in range(1, amount) if given[i] < largest] or [i for i in range(1, amount) if given[i] < most]
        pool, remaining = sum([portions[i] for i in free]), rest
        for i in free:
            addition = min(most - given[i], max(1, remaining * portions[i] // pool), rest)
            given[i] = given[i] + addition
            rest = rest - addition
    return np.array(given)


def centred(rng, dims, scale, bound, cuts=(), held_as=jnp.bfloat16):
    entries = scale * jax.random.normal(rng, dims, jnp.float32)
    if cuts:
        entries = entries * block_scale(rng, dims, cuts, -0.22, 0.18)
    return jnp.clip(entries, -bound, bound).astype(held_as)


def setup_inputs(seed: int = 0) -> dict:
    arg_keys = jax.random.split(jax.random.key(seed), 9)
    u_vel = centred(arg_keys[0], (NTILE, LEVELS, CELLS), 1.0, 6.0, ((0, 8), (1, 4)), jnp.float32)
    v_vel = centred(arg_keys[1], (NTILE, LEVELS, CELLS), 1.0, 6.0, ((0, 8), (1, 4)), jnp.float32)
    w_vel = centred(arg_keys[2], (NTILE, LEVELS, CELLS), 1.0, 6.0, ((0, 8), (1, 4)), jnp.float32)
    owner_dev_keys = jax.random.split(jax.random.fold_in(arg_keys[3], 1), NTILE * 4 // (4 * SLOTS))
    owner_dev_turns = jax.random.permutation(jax.random.fold_in(arg_keys[3], 3), NTILE * 4 // (4 * SLOTS))
    owner_dev = jax.vmap(lambda own, number: deal_out(jax.random.fold_in(arg_keys[3], 2), own, number, 4 * SLOTS, N_TILES, 1, CAP, 2))(owner_dev_keys, owner_dev_turns).reshape((NTILE, 4, 1))
    owner_slot = set_ends(jax.random.randint(arg_keys[4], (NTILE, 4), 0, SLOTS), jax.random.fold_in(arg_keys[4], 1), 0, SLOTS - 1).astype(jnp.int32)
    rotation = set_ends(jax.random.randint(arg_keys[5], (NTILE, 4), 0, 4), jax.random.fold_in(arg_keys[5], 1), 0, 3).astype(jnp.int32)
    coast = set_ends((jax.random.randint(arg_keys[6], (NTILE, 4), 0, 5) < 4).astype(jnp.int32), jax.random.fold_in(arg_keys[6], 1), 0, 1)
    live = set_ends((jax.random.randint(arg_keys[7], (NTILE,), 0, 5) < 4).astype(jnp.int32), jax.random.fold_in(arg_keys[7], 1), 0, 1)
    return {"u_vel": u_vel, "v_vel": v_vel, "w_vel": w_vel, "owner_dev": owner_dev, "owner_slot": owner_slot, "rotation": rotation, "coast": coast, "live": live}


HIGH = lax.Precision.HIGHEST


def edge_lines(values):
    return jnp.stack([values[..., :, -1], values[..., -1, :], values[..., :, 0], values[..., 0, :]], axis=-2)


def tables(length):
    index = jnp.arange(length, dtype=jnp.float32)
    phase = (2.0 * jnp.pi / length) * jnp.mod(index[:, None] * index[None, :], length)
    return jnp.cos(phase), jnp.sin(phase)


def window(length):
    places = (jnp.arange(length, dtype=jnp.float32) + 0.5) / length
    taper = 0.75 - 0.25 * jnp.cos(2.0 * jnp.pi * places)
    return taper[:, None] * taper[None, :]


def spectrum(values, cos_t, sin_t):
    with_c = jnp.einsum('bij,jl->bil', values, cos_t, precision=HIGH)
    with_s = jnp.einsum('bij,jl->bil', values, sin_t, precision=HIGH)
    real_part = jnp.einsum('ki,bil->bkl', cos_t, with_c, precision=HIGH) - jnp.einsum('ki,bil->bkl', sin_t, with_s, precision=HIGH)
    imag_part = -(jnp.einsum('ki,bil->bkl', cos_t, with_s, precision=HIGH) + jnp.einsum('ki,bil->bkl', sin_t, with_c, precision=HIGH))
    return real_part, imag_part


def turn_strips(strips, rotation, coast):
    flipped = ((rotation == 1) | (rotation == 2))[:, :, None, None, None]
    strips = jnp.where(flipped, strips[..., ::-1], strips)
    keep_sign = ((rotation == 0).astype(jnp.float32) - (rotation == 2).astype(jnp.float32))[:, :, None, None]
    swap_sign = ((rotation == 3).astype(jnp.float32) - (rotation == 1).astype(jnp.float32))[:, :, None, None]
    wetness = coast.astype(jnp.float32)[:, :, None, None]
    halo_u = wetness * (keep_sign * strips[:, :, 0] + swap_sign * strips[:, :, 1])
    halo_v = wetness * (keep_sign * strips[:, :, 1] - swap_sign * strips[:, :, 0])
    return halo_u.transpose(0, 2, 1, 3), halo_v.transpose(0, 2, 1, 3)


def horizontal(values, halo):
    east_line = halo[..., 0, :]
    north_line = halo[..., 1, :]
    west_line = halo[..., 2, :]
    south_line = halo[..., 3, :]
    slope_x = (jnp.concatenate([values[..., :, 1:], east_line[..., :, None]], -1) - jnp.concatenate([west_line[..., :, None], values[..., :, :-1]], -1)) * 0.5
    slope_y = (jnp.concatenate([values[..., 1:, :], north_line[..., None, :]], -2) - jnp.concatenate([south_line[..., None, :], values[..., :-1, :]], -2)) * 0.5
    return slope_x, slope_y


def layer_flux(shaped_u, shaped_v, shaped_w, halo_u, halo_v, depth_u, depth_v):
    tiles_here, levels_here = shaped_u.shape[0], shaped_u.shape[1]
    ux_part, uy_part = horizontal(shaped_u, halo_u)
    vx_part, vy_part = horizontal(shaped_v, halo_v)
    adv_u = shaped_u * ux_part + shaped_v * uy_part + shaped_w * depth_u
    adv_v = shaped_u * vx_part + shaped_v * vy_part + shaped_w * depth_v
    cos_t, sin_t = tables(TS)
    shade = window(TS)
    u_re, u_im = spectrum((shaped_u * shade).reshape(-1, TS, TS), cos_t, sin_t)
    v_re, v_im = spectrum((shaped_v * shade).reshape(-1, TS, TS), cos_t, sin_t)
    au_re, au_im = spectrum((adv_u * shade).reshape(-1, TS, TS), cos_t, sin_t)
    av_re, av_im = spectrum((adv_v * shade).reshape(-1, TS, TS), cos_t, sin_t)
    terms = -(u_re * au_re + u_im * au_im + v_re * av_re + v_im * av_im) / (TS * TS)
    return jnp.sum(terms.reshape(tiles_here, levels_here, TS * TS), axis=1)


def reference(u_vel, v_vel, w_vel, owner_dev, owner_slot, rotation, coast, live):
    count = u_vel.shape[0]
    levels = u_vel.shape[1]
    shaped_u = u_vel.reshape(count, levels, TS, TS)
    shaped_v = v_vel.reshape(count, levels, TS, TS)
    shaped_w = w_vel.reshape(count, levels, TS, TS)
    strips = jnp.stack([edge_lines(shaped_u), edge_lines(shaped_v)], 0).transpose(1, 3, 0, 2, 4)
    sides = jnp.arange(4, dtype=jnp.int32)
    facing = ((sides[None, :] + 2 + rotation) % 4).astype(jnp.int32)
    target = (owner_dev[:, :, 0] * SLOTS + owner_slot).astype(jnp.int32)
    picked = strips[target, facing]
    halo_u, halo_v = turn_strips(picked, rotation, coast)

    def block(index):
        start = (index * SLOTS).astype(jnp.int32)
        part_u = lax.dynamic_slice_in_dim(shaped_u, start, SLOTS, 0)
        part_v = lax.dynamic_slice_in_dim(shaped_v, start, SLOTS, 0)
        part_w = lax.dynamic_slice_in_dim(shaped_w, start, SLOTS, 0)
        part_hu = lax.dynamic_slice_in_dim(halo_u, start, SLOTS, 0)
        part_hv = lax.dynamic_slice_in_dim(halo_v, start, SLOTS, 0)
        zeros_lev = jnp.zeros((SLOTS, 1, TS, TS), jnp.float32)
        upper_u = jnp.concatenate([part_u[:, 1:], zeros_lev], 1)
        lower_u = jnp.concatenate([zeros_lev, part_u[:, :-1]], 1)
        upper_v = jnp.concatenate([part_v[:, 1:], zeros_lev], 1)
        lower_v = jnp.concatenate([zeros_lev, part_v[:, :-1]], 1)
        return layer_flux(part_u, part_v, part_w, part_hu, part_hv, (upper_u - lower_u) * 0.5, (upper_v - lower_v) * 0.5)

    flux = lax.map(block, jnp.arange(count // SLOTS, dtype=jnp.int32)).reshape(count, TS * TS)
    return flux * live.astype(jnp.float32)[:, None]
```

```python
import functools

import jax
import jax.numpy as jnp
import ml_dtypes
import numpy as np
from jax import lax
from jax.experimental import pallas as pl
from jax.experimental.pallas import tpu as pltpu
from jax.sharding import PartitionSpec as P

TS = 90
HALF = TS // 2 + 1
KP = 48
IP = 96
LN = 128
FLAT = 8192
MESH = pl.DeviceIdType.MESH
VMEM = pl.BlockSpec(memory_space=pltpu.VMEM)
BF = jnp.bfloat16


def split_np(a):
    hi = a.astype(np.float32).astype(ml_dtypes.bfloat16)
    lo = (a - hi.astype(np.float64)).astype(np.float32).astype(ml_dtypes.bfloat16)
    return hi, lo


def transform_tables():
    n = np.arange(TS)
    taper = 0.75 - 0.25 * np.cos(2 * np.pi * (n + 0.5) / TS)
    phase = 2 * np.pi * ((np.arange(HALF)[:, None] * n[None, :]) % TS) / TS
    cos_t, sin_t = np.cos(phase) * taper, np.sin(phase) * taper
    right = np.zeros((LN, LN))
    right[:TS, :HALF] = cos_t.T
    right[:TS, 64 : 64 + HALF] = sin_t.T
    hi, lo = split_np(right)
    w1 = np.block([[hi, lo], [hi, np.zeros_like(lo)]])
    left = np.zeros((2 * KP, IP))
    left[:HALF, :TS] = cos_t
    left[KP : KP + HALF, :TS] = sin_t
    hi, lo = split_np(left)
    t2 = np.block([[hi, hi], [lo, np.zeros_like(lo)]])
    return w1, t2


def expand_tables():
    fold = np.zeros((TS, HALF))
    sign = np.zeros((TS, HALF))
    for k in range(TS):
        fold[k, min(k, TS - k)] = 1
        sign[k, min(k, TS - k)] = 1 if k <= TS - k else -1
    e1 = np.zeros((LN, 2 * LN))
    e1[:HALF, :TS] = fold.T
    e1[64 : 64 + HALF, LN : LN + TS] = sign.T
    rows = np.zeros((IP, 2 * KP))
    rows[:TS, :HALF] = fold
    rows[:TS, KP : KP + HALF] = sign
    bf = ml_dtypes.bfloat16
    return np.concatenate([e1, e1], 0).astype(bf), np.concatenate([rows, rows], 1).astype(bf)


def split(x):
    hi = x.astype(BF)
    return hi, (x - hi.astype(jnp.float32)).astype(BF)


def meet(axis, n):
    me = lax.axis_index(axis)
    barrier = pltpu.get_barrier_semaphore()
    for d in range(1, n):
        pl.semaphore_signal(
            barrier, inc=1, device_id={axis: lax.rem(me + d, n)}, device_id_type=MESH
        )
    pl.semaphore_wait(barrier, n - 1)


def lines_kernel(n, uv_ref, g_ref, send_sem, recv_sem):
    me = lax.axis_index("tiles")
    rows = uv_ref.shape[0]
    lane = lax.broadcasted_iota(jnp.int32, (rows, LN), 1)

    def column(j):
        line = jnp.zeros((rows, LN), jnp.float32)
        for i in range(TS):
            c, o = divmod(TS * i + j, LN)
            turned = pltpu.roll(uv_ref[:, c * LN : (c + 1) * LN], (i - o) % LN, 1)
            line = jnp.where(lane == i, turned, line)
        return line

    g_ref[me, 0] = column(TS - 1)
    g_ref[me, 1] = uv_ref[:, TS * (TS - 1) : TS * (TS - 1) + LN]
    g_ref[me, 2] = column(0)
    g_ref[me, 3] = uv_ref[:, 0:LN]
    meet("tiles", n)
    copies = []
    for d in range(1, n):
        copy = pltpu.make_async_remote_copy(
            src_ref=g_ref.at[me],
            dst_ref=g_ref.at[me],
            send_sem=send_sem.at[d],
            recv_sem=recv_sem.at[d],
            device_id={"tiles": lax.rem(me + d, n)},
            device_id_type=MESH,
        )
        copy.start()
        copies.append(copy)
    for copy in copies:
        copy.wait()


def gather_lines(uv, n):
    rows = uv.shape[0]
    return pl.pallas_call(
        functools.partial(lines_kernel, n),
        out_shape=jax.ShapeDtypeStruct((n, 4, rows, LN), jnp.float32),
        in_specs=[VMEM],
        out_specs=VMEM,
        scratch_shapes=[pltpu.SemaphoreType.DMA((n,)), pltpu.SemaphoreType.DMA((n,))],
        compiler_params=pltpu.CompilerParams(
            collective_id=0, has_side_effects=True, vmem_limit_bytes=32 * 2**20
        ),
    )(uv)


def flux_kernel(uv_ref, w_ref, lo_ref, hi_ref, halo_ref, w1_ref, t2_ref, pq_ref, x_ref, z_ref):
    lane = lax.broadcasted_iota(jnp.int32, (8, LN), 1)

    def put(f, i, lev0, lev1):
        hi, lo = split(jnp.concatenate([lev0, lev1], 0))
        x_ref[f, 16 * i : 16 * i + 16, :LN] = hi
        x_ref[f, 16 * i : 16 * i + 16, LN:] = lo

    def line(ref, index, i):
        return ref[(*index, slice(None), slice(TS * i, TS * i + LN))]

    def centre(i):
        return [[line(uv_ref, (f, lev), i) for lev in range(2)] for f in range(2)]

    before, here = None, centre(0)
    for i in range(TS):
        after = centre(i + 1) if i < TS - 1 else None
        adv = [[None, None], [None, None]]
        for lev in range(2):
            w = line(w_ref, (lev,), i)
            for f in range(2):
                mid = here[f][lev]
                east = pltpu.roll(halo_ref[f, lev, 0], (TS - i) % LN, 1)
                west = pltpu.roll(halo_ref[f, lev, 2], (LN - 1 - i) % LN, 1)
                wide = jnp.where(lane < TS, mid, jnp.where(lane == TS, east, west))
                fx = pltpu.roll(wide, LN - 1, 1) - pltpu.roll(wide, 1, 1)
                north = after[f][lev] if i < TS - 1 else halo_ref[f, lev, 1]
                south = before[f][lev] if i > 0 else halo_ref[f, lev, 3]
                if lev == 0:
                    fz = here[f][1] - line(lo_ref, (f,), i)
                else:
                    fz = line(hi_ref, (f,), i) - here[f][0]
                adv[f][lev] = 0.5 * (
                    here[0][lev] * fx + here[1][lev] * (north - south) + w * fz
                )
        for f in range(2):
            put(f, i, *here[f])
            put(2 + f, i, *adv[f])
        before, here = here, after

    step = 288
    for f in range(4):
        z_ref[f, 16 * TS :, :] = jnp.zeros((16 * (IP - TS), LN), jnp.float32)

        def first(c, carry, f=f):
            at = pl.ds(pl.multiple_of(c * step, 16), step)
            z = jnp.dot(x_ref[f, at, :], w1_ref[...], preferred_element_type=jnp.float32)
            z_ref[f, at, :] = z[:, :LN] + z[:, LN:]
            return carry

        lax.fori_loop(0, 16 * TS // step, first, 0)

    lane_k = lax.broadcasted_iota(jnp.int32, (KP, LN), 1)

    def second(t, carry):
        p = jnp.zeros((KP, LN), jnp.float32)
        q = jnp.zeros((KP, LN), jnp.float32)
        for lev in range(2):
            for f in range(2):
                own = z_ref[f, pl.ds(8 * lev + t, IP, stride=16), :]
                adv = z_ref[2 + f, pl.ds(8 * lev + t, IP, stride=16), :]
                hi, lo = split(jnp.concatenate([own, adv], 1))
                y = jnp.dot(
                    t2_ref[...],
                    jnp.concatenate([hi, lo], 0),
                    preferred_element_type=jnp.float32,
                )
                y = y[: 2 * KP] + y[2 * KP :]
                top, bot = y[:KP, :LN], y[KP:, :LN]
                top_a, bot_a = y[:KP, LN:], y[KP:, LN:]
                p = p + top * top_a + bot * bot_a
                q = q + bot * pltpu.roll(top_a, 64, 1) - top * pltpu.roll(bot_a, 64, 1)
        pq_ref[t] = jnp.where(lane_k < 64, p + pltpu.roll(p, 64, 1), pltpu.roll(q, 64, 1) - q)
        return carry

    lax.fori_loop(0, 8, second, 0)


def partial_flux(uv, w, lo, hi, halo, w1, t2):
    slots = w.shape[1]
    whole = lambda a: pl.BlockSpec(a.shape, lambda c: (0,) * a.ndim)
    return pl.pallas_call(
        flux_kernel,
        grid=(slots // 8,),
        out_shape=jax.ShapeDtypeStruct((slots, KP, LN), jnp.float32),
        in_specs=[
            pl.BlockSpec((2, 2, 8, FLAT), lambda c: (0, 0, c, 0)),
            pl.BlockSpec((2, 8, FLAT), lambda c: (0, c, 0)),
            pl.BlockSpec((2, 8, FLAT), lambda c: (0, c, 0)),
            pl.BlockSpec((2, 8, FLAT), lambda c: (0, c, 0)),
            pl.BlockSpec((2, 2, 4, 8, LN), lambda c: (0, 0, 0, c, 0)),
            whole(w1),
            whole(t2),
        ],
        out_specs=pl.BlockSpec((8, KP, LN), lambda c: (c, 0, 0)),
        scratch_shapes=[
            pltpu.VMEM((4, 16 * TS, 2 * LN), BF),
            pltpu.VMEM((4, 16 * IP, LN), jnp.float32),
        ],
        compiler_params=pltpu.CompilerParams(vmem_limit_bytes=40 * 2**20),
    )(uv, w, lo, hi, halo, w1, t2)


def sum_kernel(n, pq_ref, scale_ref, e1_ref, rows_ref, out_ref, got, full, plane, sems):
    me = lax.axis_index("lev")
    slots = pq_ref.shape[0]
    own = slots // n
    meet("lev", n)

    def send(src, dst, stage, d):
        copy = pltpu.make_async_remote_copy(
            src_ref=src,
            dst_ref=dst,
            send_sem=sems.at[stage, 0, d],
            recv_sem=sems.at[stage, 1, d],
            device_id={"lev": lax.rem(me + d, n)},
            device_id_type=MESH,
        )
        copy.start()
        return copy

    copies = [
        send(pq_ref.at[pl.ds(lax.rem(me + d, n) * own, own)], got.at[d - 1], 0, d)
        for d in range(1, n)
    ]
    total = pq_ref[pl.ds(me * own, own)]
    for d in range(1, n):
        copies[d - 1].wait()
        total = total + got[d - 1]
    mine = full.at[pl.ds(me * own, own)]
    mine[...] = total
    copies = [send(mine, mine, 1, d) for d in range(1, n)]
    for copy in copies:
        copy.wait()

    def expand(t, carry):
        hi, lo = split(full[t])
        wide = jnp.dot(
            jnp.concatenate([hi, lo], 1), e1_ref[...], preferred_element_type=jnp.float32
        )
        hi, lo = split(jnp.concatenate([wide[:, :LN], wide[:, LN:]], 0))
        y = jnp.dot(
            rows_ref[...], jnp.concatenate([hi, lo], 0), preferred_element_type=jnp.float32
        )
        plane[pl.ds(pl.multiple_of(t * IP, 8), IP), :] = y
        return carry

    lax.fori_loop(0, slots, expand, 0)
    for k in range(TS):
        row = plane[pl.ds(k, slots, stride=IP), :] * scale_ref[...]
        out_ref[:, TS * k : TS * k + TS] = row[:, :TS]


def sum_levels(pq, scale, e1, rows, n):
    slots = pq.shape[0]
    own = slots // n
    return pl.pallas_call(
        functools.partial(sum_kernel, n),
        out_shape=jax.ShapeDtypeStruct((slots, FLAT), jnp.float32),
        in_specs=[VMEM] * 4,
        out_specs=VMEM,
        scratch_shapes=[
            pltpu.VMEM((n - 1, own, KP, LN), jnp.float32),
            pltpu.VMEM((slots, KP, LN), jnp.float32),
            pltpu.VMEM((slots * IP, LN), jnp.float32),
            pltpu.SemaphoreType.DMA((2, 2, n)),
        ],
        compiler_params=pltpu.CompilerParams(
            collective_id=1, has_side_effects=True, vmem_limit_bytes=32 * 2**20
        ),
    )(pq, scale, e1, rows)


def local(u_vel, v_vel, w_vel, owner_dev, owner_slot, rotation, coast, live):
    slots, levels, cells = u_vel.shape
    devices = lax.axis_size("tiles")
    bands = lax.axis_size("lev")
    pad = ((0, 0), (0, 0), (0, FLAT - cells))
    uv = jnp.stack([jnp.pad(x.transpose(1, 0, 2), pad) for x in (u_vel, v_vel)], 0)
    w = jnp.pad(w_vel.transpose(1, 0, 2), pad)
    up = [(i, i + 1) for i in range(bands - 1)]
    down = [(i + 1, i) for i in range(bands - 1)]
    lo = lax.ppermute(uv[:, 1], "lev", up)
    hi = lax.ppermute(uv[:, 0], "lev", down)

    lines = gather_lines(uv.reshape(4 * slots, FLAT), devices)
    sides = jnp.arange(4, dtype=jnp.int32)
    facing = (sides[None, :] + 2 + rotation) % 4
    base = (owner_dev[:, :, 0] * 4 + facing) * (4 * slots) + owner_slot
    index = (jnp.arange(4, dtype=jnp.int32) * slots)[:, None, None] + base.T[None]
    picked = lines.reshape(-1, LN)[index.reshape(-1)].reshape(2, 2, 4, slots, LN)[..., :TS]
    per_side = lambda x: x.T[None, :, :, None]
    flipped = per_side((rotation == 1) | (rotation == 2))
    picked = jnp.where(flipped[None], picked[..., ::-1], picked)
    as_f32 = lambda x: per_side(x.astype(jnp.float32))
    keep_sign = as_f32(rotation == 0) - as_f32(rotation == 2)
    swap_sign = as_f32(rotation == 3) - as_f32(rotation == 1)
    wet = as_f32(coast)
    halo = jnp.stack(
        [
            wet * (keep_sign * picked[0] + swap_sign * picked[1]),
            wet * (keep_sign * picked[1] - swap_sign * picked[0]),
        ],
        0,
    )
    halo = jnp.pad(halo, ((0, 0),) * 4 + ((0, LN - TS),))

    w1, t2 = (jnp.asarray(a) for a in transform_tables())
    e1, rows = (jnp.asarray(a) for a in expand_tables())
    pq = partial_flux(uv, w, lo, hi, halo, w1, t2)
    scale = jnp.broadcast_to(live.astype(jnp.float32)[:, None] * (-1.0 / (TS * TS)), (slots, LN))
    return sum_levels(pq, scale, e1, rows, bands)[:, :cells]


def solution(mesh):
    in_specs = (
        P("tiles", "lev", None),
        P("tiles", "lev", None),
        P("tiles", "lev", None),
        P("tiles", None, None),
        P("tiles", None),
        P("tiles", None),
        P("tiles", None),
        P("tiles"),
    )
    out_specs = P("tiles", None)
    return jax.shard_map(local, mesh=mesh, in_specs=in_specs, out_specs=out_specs, check_vma=False)
```

```python
import functools

import jax
import jax.numpy as jnp
import ml_dtypes
import numpy as np
from jax import lax
from jax.experimental import pallas as pl
from jax.experimental.pallas import tpu as pltpu
from jax.sharding import PartitionSpec as P

TS = 90
HALF = TS // 2 + 1
KP = 48
IP = 96
LN = 128
FLAT = 8192
MESH = pl.DeviceIdType.MESH
VMEM = pl.BlockSpec(memory_space=pltpu.VMEM)
BF = jnp.bfloat16


def split_np(a):
    hi = a.astype(np.float32).astype(ml_dtypes.bfloat16)
    lo = (a - hi.astype(np.float64)).astype(np.float32).astype(ml_dtypes.bfloat16)
    return hi, lo


def transform_tables():
    n = np.arange(TS)
    taper = 0.75 - 0.25 * np.cos(2 * np.pi * (n + 0.5) / TS)
    phase = 2 * np.pi * ((np.arange(HALF)[:, None] * n[None, :]) % TS) / TS
    cos_t, sin_t = np.cos(phase) * taper, np.sin(phase) * taper
    right = np.zeros((LN, LN))
    right[:TS, :HALF] = cos_t.T
    right[:TS, 64 : 64 + HALF] = sin_t.T
    hi, lo = split_np(right)
    w1 = np.block([[hi, lo], [hi, np.zeros_like(lo)]])
    left = np.zeros((2 * KP, IP))
    left[:HALF, :TS] = cos_t
    left[KP : KP + HALF, :TS] = sin_t
    hi, lo = split_np(left)
    t2 = np.block([[hi, hi], [lo, np.zeros_like(lo)]])
    return w1, t2


def expand_tables():
    fold = np.zeros((TS, HALF))
    sign = np.zeros((TS, HALF))
    for k in range(TS):
        fold[k, min(k, TS - k)] = 1
        sign[k, min(k, TS - k)] = 1 if k <= TS - k else -1
    e1 = np.zeros((LN, 2 * LN))
    e1[:HALF, :TS] = fold.T
    e1[64 : 64 + HALF, LN : LN + TS] = sign.T
    rows = np.zeros((IP, 2 * KP))
    rows[:TS, :HALF] = fold
    rows[:TS, KP : KP + HALF] = sign
    bf = ml_dtypes.bfloat16
    return np.concatenate([e1, e1], 0).astype(bf), np.concatenate([rows, rows], 1).astype(bf)


def split(x):
    hi = x.astype(BF)
    return hi, (x - hi.astype(jnp.float32)).astype(BF)


def meet(axis, n):
    me = lax.axis_index(axis)
    barrier = pltpu.get_barrier_semaphore()
    for d in range(1, n):
        pl.semaphore_signal(
            barrier, inc=1, device_id={axis: lax.rem(me + d, n)}, device_id_type=MESH
        )
    pl.semaphore_wait(barrier, n - 1)


def rows_at(ref, index, tiles, lane, i):
    c, o = divmod(TS * i, LN)

    def part(c):
        return ref[(*index, tiles, slice(c * LN, (c + 1) * LN))]

    if o == 0:
        return part(c)
    start = pltpu.roll(part(c), LN - o, 1)
    if o + TS <= LN:
        return start
    return jnp.where(lane < LN - o, start, pltpu.roll(part(c + 1), LN - o, 1))


def first_stage(x_ref, z_ref, w1_ref, f, rows):
    step = 288

    def body(c, carry):
        at = pl.ds(pl.multiple_of(c * step, 16), step)
        z = jnp.dot(x_ref[f, at, :], w1_ref[...], preferred_element_type=jnp.float32)
        z_ref[f, at, :] = z[:, :LN] + z[:, LN:]
        return carry

    z_ref[f, rows:, :] = jnp.zeros((z_ref.shape[1] - rows, LN), jnp.float32)
    lax.fori_loop(0, rows // step, body, 0)


def second_stage(z_ref, t2_ref, b, batch):
    both = [z_ref[f, pl.ds(b, IP, stride=batch), :] for f in range(2)]
    hi, lo = split(jnp.concatenate(both, 1))
    y = jnp.dot(
        t2_ref[...], jnp.concatenate([hi, lo], 0), preferred_element_type=jnp.float32
    )
    return y[: 2 * KP] + y[2 * KP :]


def exchange_kernel(
    n, bands, uv_ref, w1_ref, t2_ref, g_ref, lo_ref, hi_ref, y_ref, x_ref, z_ref, line_sems, z_sems
):
    me = lax.axis_index("tiles")
    level = lax.axis_index("lev")
    slots = uv_ref.shape[2]
    has_lo, has_hi = level > 0, level < bands - 1
    barrier = pltpu.get_barrier_semaphore()
    for d in range(1, n):
        pl.semaphore_signal(
            barrier, inc=1, device_id={"tiles": lax.rem(me + d, n)}, device_id_type=MESH
        )

    @pl.when(has_lo)
    def _():
        pl.semaphore_signal(barrier, inc=1, device_id={"lev": level - 1}, device_id_type=MESH)

    @pl.when(has_hi)
    def _():
        pl.semaphore_signal(barrier, inc=1, device_id={"lev": level + 1}, device_id_type=MESH)

    pl.semaphore_wait(
        barrier, n - 1 + jnp.minimum(level, 1) + jnp.minimum(bands - 1 - level, 1)
    )

    def level_copy(src, dst, way, f, to):
        return pltpu.make_async_remote_copy(
            src_ref=src,
            dst_ref=dst,
            send_sem=z_sems.at[way, 0, f],
            recv_sem=z_sems.at[way, 1, f],
            device_id={"lev": to},
            device_id_type=MESH,
        )

    above, below = jnp.minimum(level + 1, bands - 1), jnp.maximum(level - 1, 0)
    ups = [level_copy(uv_ref.at[f, 1], lo_ref.at[f], 0, f, above) for f in range(2)]
    downs = [level_copy(uv_ref.at[f, 0], hi_ref.at[f], 1, f, below) for f in range(2)]

    @pl.when(has_hi)
    def _():
        for copy in ups:
            copy.start()

    @pl.when(has_lo)
    def _():
        for copy in downs:
            copy.start()

    @pl.when(level == 0)
    def _():
        lo_ref[...] = jnp.zeros_like(lo_ref)

    @pl.when(level == bands - 1)
    def _():
        hi_ref[...] = jnp.zeros_like(hi_ref)

    lane = lax.broadcasted_iota(jnp.int32, (slots, LN), 1)
    for f in range(2):
        for lev in range(2):
            at = slice((2 * f + lev) * slots, (2 * f + lev + 1) * slots)

            def part(c):
                return uv_ref[f, lev, :, c * LN : (c + 1) * LN]

            east, west = part(0), part(0)
            for i in range(TS):
                c, o = divmod(TS * i + TS - 1, LN)
                turned = pltpu.roll(part(c), (i - o) % LN, 1)
                east = jnp.where(lane == i, turned, east)
                if i < TS - 1:
                    if o == LN - 1:
                        turned = pltpu.roll(part(c + 1), i + 1, 1)
                    west = jnp.where(lane == i + 1, turned, west)
            g_ref[me, 0, at] = east
            g_ref[me, 1, at] = rows_at(uv_ref, (f, lev), slice(None), lane, TS - 1)
            g_ref[me, 2, at] = west
            g_ref[me, 3, at] = part(0)
    copies = []
    for d in range(1, n):
        copy = pltpu.make_async_remote_copy(
            src_ref=g_ref.at[me],
            dst_ref=g_ref.at[me],
            send_sem=line_sems.at[0, d],
            recv_sem=line_sems.at[1, d],
            device_id={"tiles": lax.rem(me + d, n)},
            device_id_type=MESH,
        )
        copy.start()
        copies.append(copy)

    batch = 2 * slots
    for i in range(TS):
        for f in range(2):
            for lev in range(2):
                hi, lo = split(rows_at(uv_ref, (f, lev), slice(None), lane, i))
                at = batch * i + lev * slots
                x_ref[f, at : at + slots, :LN] = hi
                x_ref[f, at : at + slots, LN:] = lo
    for f in range(2):
        first_stage(x_ref, z_ref, w1_ref, f, batch * TS)

    def second(b, carry):
        y_ref[b] = second_stage(z_ref, t2_ref, b, batch)
        return carry

    lax.fori_loop(0, batch, second, 0)

    for copy in copies:
        copy.wait()

    @pl.when(has_hi)
    def _():
        for copy in ups:
            copy.wait_send()
        for copy in downs:
            copy.wait_recv()

    @pl.when(has_lo)
    def _():
        for copy in downs:
            copy.wait_send()
        for copy in ups:
            copy.wait_recv()


def exchange(uv, w1, t2, n, bands):
    slots = uv.shape[2]
    batch = 2 * slots
    shape = lambda *dims: jax.ShapeDtypeStruct(dims, jnp.float32)
    return pl.pallas_call(
        functools.partial(exchange_kernel, n, bands),
        out_shape=(
            shape(n, 4, 4 * slots, LN),
            shape(2, slots, FLAT),
            shape(2, slots, FLAT),
            shape(batch, 2 * KP, 2 * LN),
        ),
        in_specs=[VMEM] * 3,
        out_specs=(VMEM,) * 4,
        scratch_shapes=[
            pltpu.VMEM((2, batch * TS, 2 * LN), BF),
            pltpu.VMEM((2, batch * IP, LN), jnp.float32),
            pltpu.SemaphoreType.DMA((2, n)),
            pltpu.SemaphoreType.DMA((2, 2, 2)),
        ],
        compiler_params=pltpu.CompilerParams(
            collective_id=0, has_side_effects=True, vmem_limit_bytes=48 * 2**20
        ),
    )(uv, w1, t2)


def flux_kernel(
    uv_ref, w_ref, lo_ref, hi_ref, halo_ref, y0_ref, y1_ref, w1_ref, t2_ref, pq_ref, x_ref, z_ref
):
    lane = lax.broadcasted_iota(jnp.int32, (8, LN), 1)
    ends = (lane == TS - 1) | (lane == 0)
    part = TS // 3

    sides = []
    for f in range(2):
        sides.append([])
        for lev in range(2):
            east = halo_ref[f, lev, 0]
            west = pltpu.roll(halo_ref[f, lev, 2], LN - (TS - 1), 1)
            sides[f].append(
                [
                    jnp.where((lane >= part * s) & (lane < part * (s + 1)), east, -west)
                    for s in range(3)
                ]
            )

    def line(ref, index, i):
        return rows_at(ref, index, slice(None), lane, i)

    def centre(i):
        return [[line(uv_ref, (f, lev), i) for lev in range(2)] for f in range(2)]

    before, here = None, centre(0)
    for i in range(TS):
        after = centre(i + 1) if i < TS - 1 else None
        adv = [[None, None], [None, None]]
        for lev in range(2):
            w = line(w_ref, (lev,), i)
            for f in range(2):
                mid = jnp.where(lane < TS, here[f][lev], 0.0)
                beyond = pltpu.roll(sides[f][lev][i // part], (TS - 1 - i) % LN, 1)
                fx = pltpu.roll(mid, LN - 1, 1) - pltpu.roll(mid, 1, 1)
                fx = fx + jnp.where(ends, beyond, 0.0)
                north = after[f][lev] if i < TS - 1 else halo_ref[f, lev, 1]
                south = before[f][lev] if i > 0 else halo_ref[f, lev, 3]
                if lev == 0:
                    fz = here[f][1] - line(lo_ref, (f,), i)
                else:
                    fz = line(hi_ref, (f,), i) - here[f][0]
                adv[f][lev] = 0.5 * (
                    here[0][lev] * fx + here[1][lev] * (north - south) + w * fz
                )
        for f in range(2):
            hi, lo = split(jnp.concatenate(adv[f], 0))
            x_ref[f, 16 * i : 16 * i + 16, :LN] = hi
            x_ref[f, 16 * i : 16 * i + 16, LN:] = lo
        before, here = here, after

    for f in range(2):
        first_stage(x_ref, z_ref, w1_ref, f, 16 * TS)

    lane_k = lax.broadcasted_iota(jnp.int32, (KP, LN), 1)

    def second(t, carry):
        p = jnp.zeros((KP, LN), jnp.float32)
        q = jnp.zeros((KP, LN), jnp.float32)
        for lev in range(2):
            adv = second_stage(z_ref, t2_ref, 8 * lev + t, 16)
            own = (y0_ref, y1_ref)[lev]
            for f in range(2):
                at = slice(f * LN, (f + 1) * LN)
                top, bot = own[t, :KP, at], own[t, KP:, at]
                top_a, bot_a = adv[:KP, at], adv[KP:, at]
                p = p + top * top_a + bot * bot_a
                q = q + bot * pltpu.roll(top_a, 64, 1) - top * pltpu.roll(bot_a, 64, 1)
        pq_ref[t] = jnp.where(lane_k < 64, p + pltpu.roll(p, 64, 1), pltpu.roll(q, 64, 1) - q)
        return carry

    lax.fori_loop(0, 8, second, 0)


def partial_flux(uv, w, lo, hi, halo, y, w1, t2):
    slots = w.shape[1]
    steps = slots // 8
    whole = lambda a: pl.BlockSpec(a.shape, lambda c: (0,) * a.ndim)
    return pl.pallas_call(
        flux_kernel,
        grid=(steps,),
        out_shape=jax.ShapeDtypeStruct((slots, KP, LN), jnp.float32),
        in_specs=[
            pl.BlockSpec((2, 2, 8, FLAT), lambda c: (0, 0, c, 0)),
            pl.BlockSpec((2, 8, FLAT), lambda c: (0, c, 0)),
            pl.BlockSpec((2, 8, FLAT), lambda c: (0, c, 0)),
            pl.BlockSpec((2, 8, FLAT), lambda c: (0, c, 0)),
            pl.BlockSpec((2, 2, 4, 8, LN), lambda c: (0, 0, 0, c, 0)),
            pl.BlockSpec((8, 2 * KP, 2 * LN), lambda c: (c, 0, 0)),
            pl.BlockSpec((8, 2 * KP, 2 * LN), lambda c: (steps + c, 0, 0)),
            whole(w1),
            whole(t2),
        ],
        out_specs=pl.BlockSpec((8, KP, LN), lambda c: (c, 0, 0)),
        scratch_shapes=[
            pltpu.VMEM((2, 16 * TS, 2 * LN), BF),
            pltpu.VMEM((2, 16 * IP, LN), jnp.float32),
        ],
        compiler_params=pltpu.CompilerParams(vmem_limit_bytes=40 * 2**20),
    )(uv, w, lo, hi, halo, y, y, w1, t2)


def sum_kernel(n, pq_ref, scale_ref, e1_ref, rows_ref, out_ref, got, full, plane, sems):
    me = lax.axis_index("lev")
    slots = pq_ref.shape[0]
    own = slots // n
    meet("lev", n)

    def send(src, dst, stage, d):
        copy = pltpu.make_async_remote_copy(
            src_ref=src,
            dst_ref=dst,
            send_sem=sems.at[stage, 0, d],
            recv_sem=sems.at[stage, 1, d],
            device_id={"lev": lax.rem(me + d, n)},
            device_id_type=MESH,
        )
        copy.start()
        return copy

    copies = [
        send(pq_ref.at[pl.ds(lax.rem(me + d, n) * own, own)], got.at[d - 1], 0, d)
        for d in range(1, n)
    ]
    total = pq_ref[pl.ds(me * own, own)]
    for d in range(1, n):
        copies[d - 1].wait()
        total = total + got[d - 1]
    mine = full.at[pl.ds(me * own, own)]
    mine[...] = total
    copies = [send(mine, mine, 1, d) for d in range(1, n)]
    for copy in copies:
        copy.wait()

    def expand(t, carry):
        hi, lo = split(full[t])
        wide = jnp.dot(
            jnp.concatenate([hi, lo], 1), e1_ref[...], preferred_element_type=jnp.float32
        )
        hi, lo = split(jnp.concatenate([wide[:, :LN], wide[:, LN:]], 0))
        y = jnp.dot(
            rows_ref[...], jnp.concatenate([hi, lo], 0), preferred_element_type=jnp.float32
        )
        plane[pl.ds(pl.multiple_of(t * IP, 8), IP), :] = y
        return carry

    lax.fori_loop(0, slots, expand, 0)
    lane = lax.broadcasted_iota(jnp.int32, (slots, LN), 1)
    for c in range(FLAT // LN):
        chunk = jnp.zeros((slots, LN), jnp.float32)
        for k in range(c * LN // TS, min(TS, -(-(c + 1) * LN // TS))):
            shift = TS * k - c * LN
            row = pltpu.roll(plane[pl.ds(k, slots, stride=IP), :], shift % LN, 1)
            chunk = jnp.where((lane >= shift) & (lane < shift + TS), row, chunk)
        out_ref[:, c * LN : (c + 1) * LN] = chunk * scale_ref[...]


def sum_levels(pq, scale, e1, rows, n):
    slots = pq.shape[0]
    own = slots // n
    return pl.pallas_call(
        functools.partial(sum_kernel, n),
        out_shape=jax.ShapeDtypeStruct((slots, FLAT), jnp.float32),
        in_specs=[VMEM] * 4,
        out_specs=VMEM,
        scratch_shapes=[
            pltpu.VMEM((n - 1, own, KP, LN), jnp.float32),
            pltpu.VMEM((slots, KP, LN), jnp.float32),
            pltpu.VMEM((slots * IP, LN), jnp.float32),
            pltpu.SemaphoreType.DMA((2, 2, n)),
        ],
        compiler_params=pltpu.CompilerParams(
            collective_id=1, has_side_effects=True, vmem_limit_bytes=32 * 2**20
        ),
    )(pq, scale, e1, rows)


def local(u_vel, v_vel, w_vel, owner_dev, owner_slot, rotation, coast, live):
    slots, levels, cells = u_vel.shape
    devices = lax.axis_size("tiles")
    bands = lax.axis_size("lev")
    pad = ((0, 0), (0, 0), (0, FLAT - cells))
    uv = jnp.stack([jnp.pad(x.transpose(1, 0, 2), pad) for x in (u_vel, v_vel)], 0)
    w = jnp.pad(w_vel.transpose(1, 0, 2), pad)
    w1, t2 = (jnp.asarray(a) for a in transform_tables())
    e1, rows = (jnp.asarray(a) for a in expand_tables())
    lines, lo, hi, y = exchange(uv, w1, t2, devices, bands)
    sides = jnp.arange(4, dtype=jnp.int32)
    facing = (sides[None, :] + 2 + rotation) % 4
    base = (owner_dev[:, :, 0] * 4 + facing) * (4 * slots) + owner_slot
    index = (jnp.arange(4, dtype=jnp.int32) * slots)[:, None, None] + base.T[None]
    picked = lines.reshape(-1, LN)[index.reshape(-1)].reshape(2, 2, 4, slots, LN)[..., :TS]
    per_side = lambda x: x.T[None, :, :, None]
    flipped = per_side((rotation == 1) | (rotation == 2))
    picked = jnp.where(flipped[None], picked[..., ::-1], picked)
    as_f32 = lambda x: per_side(x.astype(jnp.float32))
    keep_sign = as_f32(rotation == 0) - as_f32(rotation == 2)
    swap_sign = as_f32(rotation == 3) - as_f32(rotation == 1)
    wet = as_f32(coast)
    halo = jnp.stack(
        [
            wet * (keep_sign * picked[0] + swap_sign * picked[1]),
            wet * (keep_sign * picked[1] - swap_sign * picked[0]),
        ],
        0,
    )
    halo = jnp.pad(halo, ((0, 0),) * 4 + ((0, LN - TS),))

    pq = partial_flux(uv, w, lo, hi, halo, y, w1, t2)
    scale = jnp.broadcast_to(live.astype(jnp.float32)[:, None] * (-1.0 / (TS * TS)), (slots, LN))
    return sum_levels(pq, scale, e1, rows, bands)[:, :cells]


def solution(mesh):
    in_specs = (
        P("tiles", "lev", None),
        P("tiles", "lev", None),
        P("tiles", "lev", None),
        P("tiles", None, None),
        P("tiles", None),
        P("tiles", None),
        P("tiles", None),
        P("tiles"),
    )
    out_specs = P("tiles", None)
    return jax.shard_map(local, mesh=mesh, in_specs=in_specs, out_specs=out_specs, check_vma=False)
```

```python
import functools

import jax
import jax.numpy as jnp
import ml_dtypes
import numpy as np
from jax import lax
from jax.experimental import pallas as pl
from jax.experimental.pallas import tpu as pltpu
from jax.sharding import PartitionSpec as P

TS = 90
HALF = TS // 2 + 1
KP = 48
IP = 96
LN = 128
FLAT = 8192
MESH = pl.DeviceIdType.MESH
VMEM = pl.BlockSpec(memory_space=pltpu.VMEM)
BF = jnp.bfloat16


def split_np(a):
    hi = a.astype(np.float32).astype(ml_dtypes.bfloat16)
    lo = (a - hi.astype(np.float64)).astype(np.float32).astype(ml_dtypes.bfloat16)
    return hi, lo


def transform_tables():
    n = np.arange(TS)
    taper = 0.75 - 0.25 * np.cos(2 * np.pi * (n + 0.5) / TS)
    phase = 2 * np.pi * ((np.arange(HALF)[:, None] * n[None, :]) % TS) / TS
    cos_t, sin_t = np.cos(phase) * taper, np.sin(phase) * taper
    right = np.zeros((LN, LN))
    right[:TS, :HALF] = cos_t.T
    right[:TS, 64 : 64 + HALF] = sin_t.T
    hi, lo = split_np(right)
    w1 = np.block([[hi, lo], [hi, np.zeros_like(lo)]])
    left = np.zeros((2 * KP, IP))
    left[:HALF, :TS] = cos_t
    left[KP : KP + HALF, :TS] = sin_t
    hi, lo = split_np(left)
    t2 = np.block([[hi, hi], [lo, np.zeros_like(lo)]])
    return w1, t2


def expand_tables():
    fold = np.zeros((TS, HALF))
    sign = np.zeros((TS, HALF))
    for k in range(TS):
        fold[k, min(k, TS - k)] = 1
        sign[k, min(k, TS - k)] = 1 if k <= TS - k else -1
    e1 = np.zeros((LN, 2 * LN))
    e1[:HALF, :TS] = fold.T
    e1[64 : 64 + HALF, LN : LN + TS] = sign.T
    rows = np.zeros((IP, 2 * KP))
    rows[:TS, :HALF] = fold
    rows[:TS, KP : KP + HALF] = sign
    bf = ml_dtypes.bfloat16
    return np.concatenate([e1, e1], 0).astype(bf), np.concatenate([rows, rows], 1).astype(bf)


def flip_table():
    flip = np.zeros((LN, LN))
    flip[np.arange(TS), TS - 1 - np.arange(TS)] = 1
    return np.concatenate([flip, flip], 0).astype(ml_dtypes.bfloat16)


def split(x):
    hi = x.astype(BF)
    return hi, (x - hi.astype(jnp.float32)).astype(BF)


def rows_at(ref, index, tiles, lane, i):
    c, o = divmod(TS * i, LN)

    def part(c):
        return ref[(*index, tiles, slice(c * LN, (c + 1) * LN))]

    if o == 0:
        return part(c)
    start = pltpu.roll(part(c), LN - o, 1)
    if o + TS <= LN:
        return start
    return jnp.where(lane < LN - o, start, pltpu.roll(part(c + 1), LN - o, 1))


def first_stage(x_ref, z_ref, w1_ref, f, rows):
    step = 288

    def body(c, carry):
        at = pl.ds(pl.multiple_of(c * step, 16), step)
        z = jnp.dot(x_ref[f, at, :], w1_ref[...], preferred_element_type=jnp.float32)
        z_ref[f, at, :] = z[:, :LN] + z[:, LN:]
        return carry

    z_ref[f, rows:, :] = jnp.zeros((z_ref.shape[1] - rows, LN), jnp.float32)
    lax.fori_loop(0, rows // step, body, 0)


def second_stage(z_ref, t2_ref, b, batch):
    both = [z_ref[f, pl.ds(b, IP, stride=batch), :] for f in range(2)]
    hi, lo = split(jnp.concatenate(both, 1))
    y = jnp.dot(
        t2_ref[...], jnp.concatenate([hi, lo], 0), preferred_element_type=jnp.float32
    )
    return y[: 2 * KP] + y[2 * KP :]


def whole_kernel(
    n,
    bands,
    index_ref,
    code_ref,
    scale_ref,
    uv_ref,
    w_ref,
    w1_ref,
    t2_ref,
    e1_ref,
    rows_ref,
    flip_ref,
    out_ref,
    g_ref,
    lo_ref,
    hi_ref,
    picked_ref,
    halo_ref,
    y_ref,
    x_ref,
    z_ref,
    pq_ref,
    got_ref,
    full_ref,
    plane_ref,
    line_sems,
    z_sems,
    sum_sems,
):
    me = lax.axis_index("tiles")
    level = lax.axis_index("lev")
    slots = uv_ref.shape[2]
    steps = slots // 8
    own = 8 // bands
    has_lo, has_hi = level > 0, level < bands - 1

    barrier = pltpu.get_barrier_semaphore()
    for d in range(1, n):
        pl.semaphore_signal(
            barrier, inc=1, device_id={"tiles": lax.rem(me + d, n)}, device_id_type=MESH
        )
    for d in range(1, bands):
        pl.semaphore_signal(
            barrier, inc=1, device_id={"lev": lax.rem(level + d, bands)}, device_id_type=MESH
        )
    pl.semaphore_wait(barrier, n + bands - 2)

    above, below = jnp.minimum(level + 1, bands - 1), jnp.maximum(level - 1, 0)

    def level_copy(way, f, c):
        at = pl.ds(pl.multiple_of(c * 8, 8), 8)
        return pltpu.make_async_remote_copy(
            src_ref=uv_ref.at[f, 1 - way, at],
            dst_ref=(lo_ref, hi_ref)[way].at[f, at],
            send_sem=z_sems.at[way, 0, f, c],
            recv_sem=z_sems.at[way, 1, f, c],
            device_id={"lev": (above, below)[way]},
            device_id_type=MESH,
        )

    for c in range(steps):

        @pl.when(has_hi)
        def _():
            for f in range(2):
                level_copy(0, f, c).start()

        @pl.when(has_lo)
        def _():
            for f in range(2):
                level_copy(1, f, c).start()

    @pl.when(level == 0)
    def _():
        lo_ref[...] = jnp.zeros_like(lo_ref)

    @pl.when(level == bands - 1)
    def _():
        hi_ref[...] = jnp.zeros_like(hi_ref)

    lane = lax.broadcasted_iota(jnp.int32, (slots, LN), 1)
    for f in range(2):
        for lev in range(2):
            at = slice((2 * f + lev) * slots, (2 * f + lev + 1) * slots)

            def part(c):
                return uv_ref[f, lev, :, c * LN : (c + 1) * LN]

            east, west = part(0), part(0)
            for i in range(TS):
                c, o = divmod(TS * i + TS - 1, LN)
                turned = pltpu.roll(part(c), (i - o) % LN, 1)
                east = jnp.where(lane == i, turned, east)
                if i < TS - 1:
                    if o == LN - 1:
                        turned = pltpu.roll(part(c + 1), i + 1, 1)
                    west = jnp.where(lane == i + 1, turned, west)
            g_ref[me, 0, at] = east
            g_ref[me, 1, at] = rows_at(uv_ref, (f, lev), slice(None), lane, TS - 1)
            g_ref[me, 2, at] = west
            g_ref[me, 3, at] = part(0)
    line_copies = []
    for d in range(1, n):
        copy = pltpu.make_async_remote_copy(
            src_ref=g_ref.at[me],
            dst_ref=g_ref.at[me],
            send_sem=line_sems.at[0, d],
            recv_sem=line_sems.at[1, d],
            device_id={"tiles": lax.rem(me + d, n)},
            device_id_type=MESH,
        )
        copy.start()
        line_copies.append(copy)

    batch = 2 * slots
    for i in range(TS):
        for f in range(2):
            for lev in range(2):
                hi, lo = split(rows_at(uv_ref, (f, lev), slice(None), lane, i))
                at = batch * i + lev * slots
                x_ref[f, at : at + slots, :LN] = hi
                x_ref[f, at : at + slots, LN:] = lo
    for f in range(2):
        first_stage(x_ref, z_ref, w1_ref, f, batch * TS)

    def own_spectrum(b, carry):
        y_ref[b] = second_stage(z_ref, t2_ref, b, batch)
        return carry

    lax.fori_loop(0, batch, own_spectrum, 0, unroll=2)

    for copy in line_copies:
        copy.wait()

    def pick(j, carry):
        s, t = j // slots, lax.rem(j, slots)
        source = index_ref[s, t]
        for f in range(2):
            for lev in range(2):
                picked_ref[f, lev, s, pl.ds(t, 1), :] = g_ref[
                    source // (4 * slots),
                    lax.rem(source // slots, 4),
                    pl.ds((2 * f + lev) * slots + lax.rem(source, slots), 1),
                    :,
                ]
        return carry

    lax.fori_loop(0, 4 * slots, pick, 0)
    for s in range(4):
        code = code_ref[s]
        turn = code & 3
        wet = (code >> 2).astype(jnp.float32)
        keep = wet * jnp.where(turn == 0, 1.0, jnp.where(turn == 2, -1.0, 0.0))
        swap = wet * jnp.where(turn == 3, 1.0, jnp.where(turn == 1, -1.0, 0.0))
        turned = (turn == 1) | (turn == 2)
        for lev in range(2):
            e = []
            for f in range(2):
                straight = jnp.where(lane < TS, picked_ref[f, lev, s], 0.0)
                hi, lo = split(straight)
                back = jnp.dot(
                    jnp.concatenate([hi, lo], 1),
                    flip_ref[...],
                    preferred_element_type=jnp.float32,
                )
                e.append(jnp.where(turned, back, straight))
            halo_ref[0, lev, s] = keep * e[0] + swap * e[1]
            halo_ref[1, lev, s] = keep * e[1] - swap * e[0]

    def share(c, d):
        to = lax.rem(level + d, bands)
        return pltpu.make_async_remote_copy(
            src_ref=pq_ref.at[pl.ds(c * 8 + to * own, own)],
            dst_ref=got_ref.at[c, d - 1],
            send_sem=sum_sems.at[0, 0, c, d],
            recv_sem=sum_sems.at[0, 1, c, d],
            device_id={"lev": to},
            device_id_type=MESH,
        )

    def spread(c, d):
        mine = full_ref.at[pl.ds(c * 8 + level * own, own)]
        return pltpu.make_async_remote_copy(
            src_ref=mine,
            dst_ref=mine,
            send_sem=sum_sems.at[1, 0, c, d],
            recv_sem=sum_sems.at[1, 1, c, d],
            device_id={"lev": lax.rem(level + d, bands)},
            device_id_type=MESH,
        )

    def add_up(c):
        mine = pl.ds(c * 8 + level * own, own)
        total = pq_ref[mine]
        for d in range(1, bands):
            share(c, d).wait_recv()
            total = total + got_ref[c, d - 1]
        full_ref[mine] = total
        for d in range(1, bands):
            spread(c, d).start()

    lane8 = lax.broadcasted_iota(jnp.int32, (8, LN), 1)
    ends = (lane8 == TS - 1) | (lane8 == 0)
    third = TS // 3
    lane_k = lax.broadcasted_iota(jnp.int32, (KP, LN), 1)

    def chunk(c, carry):
        tiles = pl.ds(pl.multiple_of(c * 8, 8), 8)

        @pl.when(has_lo)
        def _():
            for f in range(2):
                level_copy(0, f, c).wait_recv()

        @pl.when(has_hi)
        def _():
            for f in range(2):
                level_copy(1, f, c).wait_recv()

        sides = []
        for f in range(2):
            sides.append([])
            for lev in range(2):
                east = halo_ref[f, lev, 0, tiles]
                west = pltpu.roll(halo_ref[f, lev, 2, tiles], LN - (TS - 1), 1)
                sides[f].append(
                    [
                        jnp.where((lane8 >= third * s) & (lane8 < third * (s + 1)), east, -west)
                        for s in range(3)
                    ]
                )

        def line(ref, index, i):
            return rows_at(ref, index, tiles, lane8, i)

        def centre(i):
            return [[line(uv_ref, (f, lev), i) for lev in range(2)] for f in range(2)]

        before, here = None, centre(0)
        for i in range(TS):
            after = centre(i + 1) if i < TS - 1 else None
            adv = [[None, None], [None, None]]
            for lev in range(2):
                w = line(w_ref, (lev,), i)
                for f in range(2):
                    mid = jnp.where(lane8 < TS, here[f][lev], 0.0)
                    beyond = pltpu.roll(sides[f][lev][i // third], (TS - 1 - i) % LN, 1)
                    fx = pltpu.roll(mid, LN - 1, 1) - pltpu.roll(mid, 1, 1)
                    fx = fx + jnp.where(ends, beyond, 0.0)
                    north = after[f][lev] if i < TS - 1 else halo_ref[f, lev, 1, tiles]
                    south = before[f][lev] if i > 0 else halo_ref[f, lev, 3, tiles]
                    if lev == 0:
                        fz = here[f][1] - line(lo_ref, (f,), i)
                    else:
                        fz = line(hi_ref, (f,), i) - here[f][0]
                    adv[f][lev] = 0.5 * (
                        here[0][lev] * fx + here[1][lev] * (north - south) + w * fz
                    )
            for f in range(2):
                hi, lo = split(jnp.concatenate(adv[f], 0))
                x_ref[f, 16 * i : 16 * i + 16, :LN] = hi
                x_ref[f, 16 * i : 16 * i + 16, LN:] = lo
            before, here = here, after

        for f in range(2):
            first_stage(x_ref, z_ref, w1_ref, f, 16 * TS)

        @pl.when(c > 0)
        def _():
            add_up(c - 1)

        def second(t, carry):
            p = jnp.zeros((KP, LN), jnp.float32)
            q = jnp.zeros((KP, LN), jnp.float32)
            for lev in range(2):
                adv = second_stage(z_ref, t2_ref, 8 * lev + t, 16)
                b = lev * slots + c * 8 + t
                for f in range(2):
                    at = slice(f * LN, (f + 1) * LN)
                    top, bot = y_ref[b, :KP, at], y_ref[b, KP:, at]
                    top_a, bot_a = adv[:KP, at], adv[KP:, at]
                    p = p + top * top_a + bot * bot_a
                    q = q + bot * pltpu.roll(top_a, 64, 1) - top * pltpu.roll(bot_a, 64, 1)
            pq_ref[c * 8 + t] = jnp.where(
                lane_k < 64, p + pltpu.roll(p, 64, 1), pltpu.roll(q, 64, 1) - q
            )
            return carry

        lax.fori_loop(0, 8, second, 0)
        for d in range(1, bands):
            share(c, d).start()
        return carry

    lax.fori_loop(0, steps, chunk, 0)
    add_up(steps - 1)

    def expand(t, carry):
        hi, lo = split(full_ref[t])
        wide = jnp.dot(
            jnp.concatenate([hi, lo], 1), e1_ref[...], preferred_element_type=jnp.float32
        )
        hi, lo = split(jnp.concatenate([wide[:, :LN], wide[:, LN:]], 0))
        y = jnp.dot(
            rows_ref[...], jnp.concatenate([hi, lo], 0), preferred_element_type=jnp.float32
        )
        plane_ref[pl.ds(pl.multiple_of(t * IP, 8), IP), :] = y
        return carry

    for c in range(steps):
        for d in range(1, bands):
            spread(c, d).wait_recv()
        lax.fori_loop(8 * c, 8 * c + 8, expand, 0, unroll=2)
    for c in range(FLAT // LN):
        piece = jnp.zeros((slots, LN), jnp.float32)
        for k in range(c * LN // TS, min(TS, -(-(c + 1) * LN // TS))):
            shift = TS * k - c * LN
            row = pltpu.roll(plane_ref[pl.ds(k, slots, stride=IP), :], shift % LN, 1)
            piece = jnp.where((lane >= shift) & (lane < shift + TS), row, piece)
        out_ref[:, c * LN : (c + 1) * LN] = piece * scale_ref[...]

    for c in range(steps):

        @pl.when(has_hi)
        def _():
            for f in range(2):
                level_copy(0, f, c).wait_send()

        @pl.when(has_lo)
        def _():
            for f in range(2):
                level_copy(1, f, c).wait_send()

        for d in range(1, bands):
            share(c, d).wait_send()
            spread(c, d).wait_send()


def whole(index, code, scale, uv, w, n, bands):
    slots = uv.shape[2]
    batch = 2 * slots
    steps = slots // 8
    w1, t2 = transform_tables()
    e1, rows = expand_tables()
    tables = [jnp.asarray(a) for a in (w1, t2, e1, rows, flip_table())]
    f32 = lambda *dims: pltpu.VMEM(dims, jnp.float32)
    return pl.pallas_call(
        functools.partial(whole_kernel, n, bands),
        out_shape=jax.ShapeDtypeStruct((slots, FLAT), jnp.float32),
        in_specs=[pl.BlockSpec(memory_space=pltpu.SMEM)] + [VMEM] * 9,
        out_specs=VMEM,
        scratch_shapes=[
            f32(n, 4, 4 * slots, LN),
            f32(2, slots, FLAT),
            f32(2, slots, FLAT),
            f32(2, 2, 4, slots, LN),
            f32(2, 2, 4, slots, LN),
            f32(batch, 2 * KP, 2 * LN),
            pltpu.VMEM((2, batch * TS, 2 * LN), BF),
            f32(2, batch * IP, LN),
            f32(slots, KP, LN),
            f32(steps, bands - 1, 8 // bands, KP, LN),
            f32(slots, KP, LN),
            f32(slots * IP, LN),
            pltpu.SemaphoreType.DMA((2, n)),
            pltpu.SemaphoreType.DMA((2, 2, 2, steps)),
            pltpu.SemaphoreType.DMA((2, 2, steps, bands)),
        ],
        compiler_params=pltpu.CompilerParams(
            collective_id=0, has_side_effects=True, vmem_limit_bytes=48 * 2**20
        ),
    )(index, code, scale, uv, w, *tables)


def local(u_vel, v_vel, w_vel, owner_dev, owner_slot, rotation, coast, live):
    slots, levels, cells = u_vel.shape
    pad = ((0, 0), (0, 0), (0, FLAT - cells))
    uv = jnp.stack([jnp.pad(x.transpose(1, 0, 2), pad) for x in (u_vel, v_vel)], 0)
    w = jnp.pad(w_vel.transpose(1, 0, 2), pad)
    facing = (jnp.arange(4, dtype=jnp.int32)[None, :] + 2 + rotation) % 4
    index = ((owner_dev[:, :, 0] * 4 + facing) * slots + owner_slot).T
    code = jnp.broadcast_to((rotation + 4 * coast).T[:, :, None], (4, slots, LN))
    scale = jnp.broadcast_to(live.astype(jnp.float32)[:, None] * (-1.0 / (TS * TS)), (slots, LN))
    n, bands = lax.axis_size("tiles"), lax.axis_size("lev")
    return whole(index, code, scale, uv, w, n, bands)[:, :cells]


def solution(mesh):
    in_specs = (
        P("tiles", "lev", None),
        P("tiles", "lev", None),
        P("tiles", "lev", None),
        P("tiles", None, None),
        P("tiles", None),
        P("tiles", None),
        P("tiles", None),
        P("tiles"),
    )
    out_specs = P("tiles", None)
    return jax.shard_map(local, mesh=mesh, in_specs=in_specs, out_specs=out_specs, check_vma=False)
```

```python
import functools

import jax
import jax.numpy as jnp
import ml_dtypes
import numpy as np
from jax import lax
from jax.experimental import pallas as pl
from jax.experimental.pallas import tpu as pltpu
from jax.sharding import PartitionSpec as P

TS = 90
HALF = TS // 2 + 1
KP = 48
IP = 96
LN = 128
FLAT = 8192
MESH = pl.DeviceIdType.MESH
VMEM = pl.BlockSpec(memory_space=pltpu.VMEM)
BF = jnp.bfloat16


def split_np(a):
    hi = a.astype(np.float32).astype(ml_dtypes.bfloat16)
    lo = (a - hi.astype(np.float64)).astype(np.float32).astype(ml_dtypes.bfloat16)
    return hi, lo


def transform_tables():
    n = np.arange(TS)
    taper = 0.75 - 0.25 * np.cos(2 * np.pi * (n + 0.5) / TS)
    phase = 2 * np.pi * ((np.arange(HALF)[:, None] * n[None, :]) % TS) / TS
    cos_t, sin_t = np.cos(phase) * taper, np.sin(phase) * taper
    right = np.zeros((LN, LN))
    right[:TS, :HALF] = cos_t.T
    right[:TS, 64 : 64 + HALF] = sin_t.T
    hi, lo = split_np(right)
    w1 = np.block([[hi, lo], [hi, np.zeros_like(lo)]])
    left = np.zeros((2 * KP, IP))
    left[:HALF, :TS] = cos_t
    left[KP : KP + HALF, :TS] = sin_t
    hi, lo = split_np(left)
    t2 = np.block([[hi, hi], [lo, np.zeros_like(lo)]])
    return w1, t2


def expand_tables():
    fold = np.zeros((TS, HALF))
    sign = np.zeros((TS, HALF))
    for k in range(TS):
        fold[k, min(k, TS - k)] = 1
        sign[k, min(k, TS - k)] = 1 if k <= TS - k else -1
    e1 = np.zeros((LN, 2 * LN))
    e1[:HALF, :TS] = fold.T
    e1[64 : 64 + HALF, LN : LN + TS] = sign.T
    rows = np.zeros((IP, 2 * KP))
    rows[:TS, :HALF] = fold
    rows[:TS, KP : KP + HALF] = sign
    bf = ml_dtypes.bfloat16
    return np.concatenate([e1, e1], 0).astype(bf), np.concatenate([rows, rows], 1).astype(bf)


def flip_table():
    flip = np.zeros((LN, LN))
    flip[np.arange(TS), TS - 1 - np.arange(TS)] = 1
    return np.concatenate([flip, flip], 0).astype(ml_dtypes.bfloat16)


def split(x):
    hi = x.astype(BF)
    return hi, (x - hi.astype(jnp.float32)).astype(BF)


def rows_at(ref, index, tiles, lane, i):
    c, o = divmod(TS * i, LN)

    def part(c):
        return ref[(*index, tiles, slice(c * LN, (c + 1) * LN))]

    if o == 0:
        return part(c)
    start = pltpu.roll(part(c), LN - o, 1)
    if o + TS <= LN:
        return start
    return jnp.where(lane < LN - o, start, pltpu.roll(part(c + 1), LN - o, 1))


def first_stage(x_ref, z_ref, w1_ref, f, rows):
    step = 288

    def body(c, carry):
        at = pl.ds(pl.multiple_of(c * step, 16), step)
        z = jnp.dot(x_ref[f, at, :], w1_ref[...], preferred_element_type=jnp.float32)
        z_ref[f, at, :] = z[:, :LN] + z[:, LN:]
        return carry

    z_ref[f, rows:, :] = jnp.zeros((z_ref.shape[1] - rows, LN), jnp.float32)
    lax.fori_loop(0, rows // step, body, 0)


def second_stage(z_ref, t2_ref, b, batch):
    both = [z_ref[f, pl.ds(b, IP, stride=batch), :] for f in range(2)]
    hi, lo = split(jnp.concatenate(both, 1))
    y = jnp.dot(
        t2_ref[...], jnp.concatenate([hi, lo], 0), preferred_element_type=jnp.float32
    )
    return y[: 2 * KP] + y[2 * KP :]


def whole_kernel(
    n,
    bands,
    index_ref,
    code_ref,
    scale_ref,
    uv_ref,
    w_ref,
    w1_ref,
    t2_ref,
    e1_ref,
    rows_ref,
    flip_ref,
    out_ref,
    g_ref,
    lo_ref,
    hi_ref,
    picked_ref,
    halo_ref,
    y_ref,
    x_ref,
    z_ref,
    pq_ref,
    got_ref,
    full_ref,
    plane_ref,
    line_sems,
    z_sems,
    sum_sems,
):
    me = lax.axis_index("tiles")
    level = lax.axis_index("lev")
    slots = uv_ref.shape[2]
    steps = slots // 8
    own = 8 // bands
    has_lo, has_hi = level > 0, level < bands - 1

    barrier = pltpu.get_barrier_semaphore()
    for d in range(1, n):
        pl.semaphore_signal(
            barrier, inc=1, device_id={"tiles": lax.rem(me + d, n)}, device_id_type=MESH
        )
    for d in range(1, bands):
        pl.semaphore_signal(
            barrier, inc=1, device_id={"lev": lax.rem(level + d, bands)}, device_id_type=MESH
        )
    pl.semaphore_wait(barrier, n + bands - 2)

    above, below = jnp.minimum(level + 1, bands - 1), jnp.maximum(level - 1, 0)

    def level_copy(way, f, c):
        at = pl.ds(pl.multiple_of(c * 8, 8), 8)
        return pltpu.make_async_remote_copy(
            src_ref=uv_ref.at[f, 1 - way, at],
            dst_ref=(lo_ref, hi_ref)[way].at[f, at],
            send_sem=z_sems.at[way, 0, f, c],
            recv_sem=z_sems.at[way, 1, f, c],
            device_id={"lev": (above, below)[way]},
            device_id_type=MESH,
        )

    for c in range(steps):

        @pl.when(has_hi)
        def _():
            for f in range(2):
                level_copy(0, f, c).start()

        @pl.when(has_lo)
        def _():
            for f in range(2):
                level_copy(1, f, c).start()

    @pl.when(level == 0)
    def _():
        lo_ref[...] = jnp.zeros_like(lo_ref)

    @pl.when(level == bands - 1)
    def _():
        hi_ref[...] = jnp.zeros_like(hi_ref)

    lane = lax.broadcasted_iota(jnp.int32, (slots, LN), 1)
    for f in range(2):
        for lev in range(2):
            at = slice((2 * f + lev) * slots, (2 * f + lev + 1) * slots)

            def part(c):
                return uv_ref[f, lev, :, c * LN : (c + 1) * LN]

            east, west = part(0), part(0)
            for i in range(TS):
                c, o = divmod(TS * i + TS - 1, LN)
                turned = pltpu.roll(part(c), (i - o) % LN, 1)
                east = jnp.where(lane == i, turned, east)
                if i < TS - 1:
                    if o == LN - 1:
                        turned = pltpu.roll(part(c + 1), i + 1, 1)
                    west = jnp.where(lane == i + 1, turned, west)
            g_ref[me, 0, at] = east
            g_ref[me, 1, at] = rows_at(uv_ref, (f, lev), slice(None), lane, TS - 1)
            g_ref[me, 2, at] = west
            g_ref[me, 3, at] = part(0)
    line_copies = []
    for d in range(1, n):
        copy = pltpu.make_async_remote_copy(
            src_ref=g_ref.at[me],
            dst_ref=g_ref.at[me],
            send_sem=line_sems.at[0, d],
            recv_sem=line_sems.at[1, d],
            device_id={"tiles": lax.rem(me + d, n)},
            device_id_type=MESH,
        )
        copy.start()
        line_copies.append(copy)

    batch = 2 * slots
    for i in range(TS):
        for f in range(2):
            for lev in range(2):
                hi, lo = split(rows_at(uv_ref, (f, lev), slice(None), lane, i))
                at = batch * i + lev * slots
                x_ref[f, at : at + slots, :LN] = hi
                x_ref[f, at : at + slots, LN:] = lo
    for f in range(2):
        first_stage(x_ref, z_ref, w1_ref, f, batch * TS)

    def own_spectrum(b, carry):
        y_ref[b] = second_stage(z_ref, t2_ref, b, batch)
        return carry

    lax.fori_loop(0, batch, own_spectrum, 0, unroll=2)

    for copy in line_copies:
        copy.wait()

    def pick(j, carry):
        s, t = j // slots, lax.rem(j, slots)
        source = index_ref[s, t]
        for f in range(2):
            for lev in range(2):
                picked_ref[f, lev, s, pl.ds(t, 1), :] = g_ref[
                    source // (4 * slots),
                    lax.rem(source // slots, 4),
                    pl.ds((2 * f + lev) * slots + lax.rem(source, slots), 1),
                    :,
                ]
        return carry

    lax.fori_loop(0, 4 * slots, pick, 0)
    for s in range(4):
        code = code_ref[s]
        turn = code & 3
        wet = (code >> 2).astype(jnp.float32)
        keep = wet * jnp.where(turn == 0, 1.0, jnp.where(turn == 2, -1.0, 0.0))
        swap = wet * jnp.where(turn == 3, 1.0, jnp.where(turn == 1, -1.0, 0.0))
        turned = (turn == 1) | (turn == 2)
        for lev in range(2):
            e = []
            for f in range(2):
                straight = jnp.where(lane < TS, picked_ref[f, lev, s], 0.0)
                hi, lo = split(straight)
                back = jnp.dot(
                    jnp.concatenate([hi, lo], 1),
                    flip_ref[...],
                    preferred_element_type=jnp.float32,
                )
                e.append(jnp.where(turned, back, straight))
            halo_ref[0, lev, s] = keep * e[0] + swap * e[1]
            halo_ref[1, lev, s] = keep * e[1] - swap * e[0]

    def share(c, d):
        to = lax.rem(level + d, bands)
        return pltpu.make_async_remote_copy(
            src_ref=pq_ref.at[pl.ds(c * 8 + to * own, own)],
            dst_ref=got_ref.at[c, d - 1],
            send_sem=sum_sems.at[0, 0, c, d],
            recv_sem=sum_sems.at[0, 1, c, d],
            device_id={"lev": to},
            device_id_type=MESH,
        )

    def spread(c, d):
        mine = full_ref.at[pl.ds(c * 8 + level * own, own)]
        return pltpu.make_async_remote_copy(
            src_ref=mine,
            dst_ref=mine,
            send_sem=sum_sems.at[1, 0, c, d],
            recv_sem=sum_sems.at[1, 1, c, d],
            device_id={"lev": lax.rem(level + d, bands)},
            device_id_type=MESH,
        )

    def add_up(c):
        mine = pl.ds(c * 8 + level * own, own)
        total = pq_ref[mine]
        for d in range(1, bands):
            share(c, d).wait_recv()
            total = total + got_ref[c, d - 1]
        full_ref[mine] = total
        for d in range(1, bands):
            spread(c, d).start()

    lane8 = lax.broadcasted_iota(jnp.int32, (8, LN), 1)
    ends = (lane8 == TS - 1) | (lane8 == 0)
    third = TS // 3
    lane_k = lax.broadcasted_iota(jnp.int32, (KP, LN), 1)

    def chunk(c, carry):
        tiles = pl.ds(pl.multiple_of(c * 8, 8), 8)

        @pl.when(has_lo)
        def _():
            for f in range(2):
                level_copy(0, f, c).wait_recv()

        @pl.when(has_hi)
        def _():
            for f in range(2):
                level_copy(1, f, c).wait_recv()

        sides = []
        for f in range(2):
            sides.append([])
            for lev in range(2):
                east = halo_ref[f, lev, 0, tiles]
                west = pltpu.roll(halo_ref[f, lev, 2, tiles], LN - (TS - 1), 1)
                sides[f].append(
                    [
                        jnp.where((lane8 >= third * s) & (lane8 < third * (s + 1)), east, -west)
                        for s in range(3)
                    ]
                )

        def line(ref, index, i):
            return rows_at(ref, index, tiles, lane8, i)

        def centre(i):
            return [[line(uv_ref, (f, lev), i) for lev in range(2)] for f in range(2)]

        before, here = None, centre(0)
        for i in range(TS):
            after = centre(i + 1) if i < TS - 1 else None
            adv = [[None, None], [None, None]]
            for lev in range(2):
                w = line(w_ref, (lev,), i)
                for f in range(2):
                    mid = jnp.where(lane8 < TS, here[f][lev], 0.0)
                    beyond = pltpu.roll(sides[f][lev][i // third], (TS - 1 - i) % LN, 1)
                    fx = pltpu.roll(mid, LN - 1, 1) - pltpu.roll(mid, 1, 1)
                    fx = fx + jnp.where(ends, beyond, 0.0)
                    north = after[f][lev] if i < TS - 1 else halo_ref[f, lev, 1, tiles]
                    south = before[f][lev] if i > 0 else halo_ref[f, lev, 3, tiles]
                    if lev == 0:
                        fz = here[f][1] - line(lo_ref, (f,), i)
                    else:
                        fz = line(hi_ref, (f,), i) - here[f][0]
                    adv[f][lev] = 0.5 * (
                        here[0][lev] * fx + here[1][lev] * (north - south) + w * fz
                    )
            for f in range(2):
                hi, lo = split(jnp.concatenate(adv[f], 0))
                x_ref[f, 16 * i : 16 * i + 16, :LN] = hi
                x_ref[f, 16 * i : 16 * i + 16, LN:] = lo
            before, here = here, after

        @pl.when(c > 0)
        def _():
            add_up(c - 1)

        for f in range(2):
            first_stage(x_ref, z_ref, w1_ref, f, 16 * TS)

        def second(t, carry):
            p = jnp.zeros((KP, LN), jnp.float32)
            q = jnp.zeros((KP, LN), jnp.float32)
            for lev in range(2):
                adv = second_stage(z_ref, t2_ref, 8 * lev + t, 16)
                b = lev * slots + c * 8 + t
                for f in range(2):
                    at = slice(f * LN, (f + 1) * LN)
                    top, bot = y_ref[b, :KP, at], y_ref[b, KP:, at]
                    top_a, bot_a = adv[:KP, at], adv[KP:, at]
                    p = p + top * top_a + bot * bot_a
                    q = q + bot * pltpu.roll(top_a, 64, 1) - top * pltpu.roll(bot_a, 64, 1)
            pq_ref[c * 8 + t] = jnp.where(
                lane_k < 64, p + pltpu.roll(p, 64, 1), pltpu.roll(q, 64, 1) - q
            )
            return carry

        for d in (*range(1, bands), 0):
            start = lax.rem(level + d, bands) * own
            lax.fori_loop(start, start + own, second, 0)
            if d:
                share(c, d).start()
        return carry

    lax.fori_loop(0, steps, chunk, 0)

    def expand(first):
        hi, lo = split(full_ref[pl.ds(first, own)].reshape(own * KP, LN))
        wide = jnp.dot(
            jnp.concatenate([hi, lo], 1), e1_ref[...], preferred_element_type=jnp.float32
        )
        even, odd = wide[:, :LN], wide[:, LN:]
        both = [
            jnp.concatenate([x[KP * t : KP * (t + 1)] for x in (even, odd)], 0)
            for t in range(own)
        ]
        hi, lo = split(jnp.concatenate(both, 1))
        y = jnp.dot(
            rows_ref[...], jnp.concatenate([hi, lo], 0), preferred_element_type=jnp.float32
        )
        for t in range(own):
            at = pl.ds(pl.multiple_of((first + t) * IP, 8), IP)
            plane_ref[at, :] = y[:, LN * t : LN * (t + 1)]

    def finish(step):
        for d in range(bands):
            if d:
                spread(step, d).wait_recv()
            expand(8 * step + lax.rem(level + bands - d, bands) * own)
        at = slice(8 * step, 8 * step + 8)
        for c in range(FLAT // LN):
            piece = jnp.zeros((8, LN), jnp.float32)
            for k in range(c * LN // TS, min(TS, -(-(c + 1) * LN // TS))):
                shift = TS * k - c * LN
                row = plane_ref[pl.ds(8 * step * IP + k, 8, stride=IP), :]
                row = pltpu.roll(row, shift % LN, 1)
                piece = jnp.where((lane8 >= shift) & (lane8 < shift + TS), row, piece)
            out_ref[at, c * LN : (c + 1) * LN] = piece * scale_ref[at]

    for step in range(steps - 1):
        finish(step)
    add_up(steps - 1)
    finish(steps - 1)

    for c in range(steps):

        @pl.when(has_hi)
        def _():
            for f in range(2):
                level_copy(0, f, c).wait_send()

        @pl.when(has_lo)
        def _():
            for f in range(2):
                level_copy(1, f, c).wait_send()

        for d in range(1, bands):
            share(c, d).wait_send()
            spread(c, d).wait_send()


def whole(index, code, scale, uv, w, n, bands):
    slots = uv.shape[2]
    batch = 2 * slots
    steps = slots // 8
    w1, t2 = transform_tables()
    e1, rows = expand_tables()
    tables = [jnp.asarray(a) for a in (w1, t2, e1, rows, flip_table())]
    f32 = lambda *dims: pltpu.VMEM(dims, jnp.float32)
    return pl.pallas_call(
        functools.partial(whole_kernel, n, bands),
        out_shape=jax.ShapeDtypeStruct((slots, FLAT), jnp.float32),
        in_specs=[pl.BlockSpec(memory_space=pltpu.SMEM)] + [VMEM] * 9,
        out_specs=VMEM,
        scratch_shapes=[
            f32(n, 4, 4 * slots, LN),
            f32(2, slots, FLAT),
            f32(2, slots, FLAT),
            f32(2, 2, 4, slots, LN),
            f32(2, 2, 4, slots, LN),
            f32(batch, 2 * KP, 2 * LN),
            pltpu.VMEM((2, batch * TS, 2 * LN), BF),
            f32(2, batch * IP, LN),
            f32(slots, KP, LN),
            f32(steps, bands - 1, 8 // bands, KP, LN),
            f32(slots, KP, LN),
            f32(slots * IP, LN),
            pltpu.SemaphoreType.DMA((2, n)),
            pltpu.SemaphoreType.DMA((2, 2, 2, steps)),
            pltpu.SemaphoreType.DMA((2, 2, steps, bands)),
        ],
        compiler_params=pltpu.CompilerParams(
            collective_id=0, has_side_effects=True, vmem_limit_bytes=48 * 2**20
        ),
    )(index, code, scale, uv, w, *tables)


def local(u_vel, v_vel, w_vel, owner_dev, owner_slot, rotation, coast, live):
    slots, levels, cells = u_vel.shape
    pad = ((0, 0), (0, 0), (0, FLAT - cells))
    uv = jnp.stack([jnp.pad(x.transpose(1, 0, 2), pad) for x in (u_vel, v_vel)], 0)
    w = jnp.pad(w_vel.transpose(1, 0, 2), pad)
    facing = (jnp.arange(4, dtype=jnp.int32)[None, :] + 2 + rotation) % 4
    index = ((owner_dev[:, :, 0] * 4 + facing) * slots + owner_slot).T
    code = jnp.broadcast_to((rotation + 4 * coast).T[:, :, None], (4, slots, LN))
    scale = jnp.broadcast_to(live.astype(jnp.float32)[:, None] * (-1.0 / (TS * TS)), (slots, LN))
    n, bands = lax.axis_size("tiles"), lax.axis_size("lev")
    return whole(index, code, scale, uv, w, n, bands)[:, :cells]


def solution(mesh):
    in_specs = (
        P("tiles", "lev", None),
        P("tiles", "lev", None),
        P("tiles", "lev", None),
        P("tiles", None, None),
        P("tiles", None),
        P("tiles", None),
        P("tiles", None),
        P("tiles"),
    )
    out_specs = P("tiles", None)
    return jax.shard_map(local, mesh=mesh, in_specs=in_specs, out_specs=out_specs, check_vma=False)
```
